256 devices in a mesh: aux: 8 (over z), pair: 32 (over x, y, core).
Axes of the slice: x: 4, y: 4, z: 8, core: 2. Of those that a mesh axis runs over, the one named last changes fastest.
Arguments:
- b_three: bfloat16 [16384, 4096], P('pair', 'aux'), may hold values from -0.09375 to 0.09375
- metric: bfloat16 [4096, 4096], P(None, 'aux'), may hold values from -1 to 2
- aux_map: int32 [256, 64], P('pair', 'aux'), may hold values 0 or 1
- domains: int32 [320, 4], replicated, may hold values from 0 to 255, as said below
- counts: int32 [320], P('pair'), may hold values from 1 to 4, as said below
Outputs:
- pair_integrals: float32 [320, 256, 256], P('pair', 'aux')
The draws below stay inside these ranges and needn't reach their ends.
Inputs may be any that keep to these rules, and one draw needn't show every extreme that they name: `domains`: of the 40 slots of the pairs of one index of pair (pairs q * 10 to (q + 1) * 10 - 1), at most 2 name blocks held by one index of pair (blocks o * 8 to (o + 1) * 8 - 1), and exactly 2 for some such index in every draw. `counts`: slots at or past a pair's count are padding.
All inputs are finite; a program needn't handle non-finite values. No bound on the sum of `aux_map` on one device may be relied on, other than what follows from the above.
Results may differ from the reference program's by a relative error of at most 0.00079.
Values may be sent and summed in bfloat16 or wider, within the bound.
No kernel may reach another device: no remote copies, remote signals or barrier semaphores. Data moves between devices by JAX's collectives and lax.ppermute only.
A program may use at most 64 MiB of HBM per device.

```python
import jax
import jax.numpy as jnp
from jax import lax

AUXW = 64
CW = 64
DMAX = 4
DB_DEV = 8
PAIR_DEV = 10
NAB = 64
NA = 4096
NDB = 256
NPAIRS = 320
SLOTS = 40
CAP = 2
N_PAIR = 32


def draw_metric(key, part):
    noise = jax.random.normal(key, (NA, NA), jnp.float32)
    return (jnp.eye(NA, dtype=jnp.float32) + 0.5 * noise * NA ** (-0.5)).astype(jnp.bfloat16)


def draw_domains(key, part):
    device_keys = jax.random.split(jax.random.fold_in(key, 11), N_PAIR)

    def one_device(sub_key):
        shuffled = jax.random.permutation(sub_key, CAP * N_PAIR)
        return (shuffled[:SLOTS] % N_PAIR).astype(jnp.int32)
    owners = jax.vmap(one_device)(device_keys)
    local_block = jax.random.randint(jax.random.fold_in(key, 12), (N_PAIR, SLOTS), 0, DB_DEV)
    return (owners * DB_DEV + local_block).reshape(NPAIRS, DMAX).astype(jnp.int32)


def draw_counts(key, part):
    device_level = jax.random.randint(jax.random.fold_in(key, 21), (N_PAIR, 1), 1, DMAX + 1)
    raw_counts = jax.random.randint(jax.random.fold_in(key, 22), (N_PAIR, PAIR_DEV), 1, DMAX + 1)
    counts = jnp.minimum(raw_counts, device_level).reshape(NPAIRS)
    full_pair = jax.random.randint(jax.random.fold_in(key, 23), (), 0, NPAIRS)
    return counts.at[full_pair].set(DMAX).astype(jnp.int32)


def place_ends(result, rng, smallest, largest):
    longest = result.shape.index(max(result.shape))
    spots = []
    for shift in (0, 1):
        where = [jax.random.randint(jax.random.fold_in(rng, axis), (), 0, length) for axis, length in enumerate(result.shape)]
        where[longest] = (where[longest] + shift) % result.shape[longest]
        spots.append(tuple(where))
    return result.at[spots[0]].set(smallest).at[spots[1]].set(largest)


def shard_levels(own_key, shape, pieces, low, largest):
    gain = 1.0
    for dim, shards_of in pieces:
        draws = jax.random.uniform(jax.random.fold_in(jax.random.fold_in(own_key, 6), dim), (shards_of,), jnp.float32, low / len(pieces), largest / len(pieces))
        gain = gain * jnp.repeat(jnp.exp(draws), shape[dim] // shards_of).reshape((-1,) + (1,) * (len(shape) - 1 - dim))
    return gain


def gaussian(key, shape, width, most, cuts=(), kind=jnp.bfloat16):
    entries = jax.random.normal(key, shape, jnp.float32) * width
    if len(cuts) > 0:
        entries = shard_levels(key, shape, cuts, -0.22, 0.18) * entries
    return jnp.clip(entries, min=-most, max=most).astype(kind)


def setup_inputs(seed: int = 0) -> dict:
    keys = jax.random.split(jax.random.key(seed), 6)
    return {
        "b_three": gaussian(keys[0], (NDB * CW, NA), (NA ** -0.5), 0.09375, ((0, 32), (1, 8))),
        "metric": draw_metric(jax.random.fold_in(keys[5], 71), 0),
        "aux_map": place_ends((jax.random.randint(keys[2], (NDB, NAB), 0, 4) < 3).astype(jnp.int32), jax.random.fold_in(keys[2], 1), 0, 1),
        "domains": draw_domains(jax.random.fold_in(keys[5], 71), 0),
        "counts": draw_counts(jax.random.fold_in(keys[5], 71), 0),
    }


def reference(b_three, metric, aux_map, domains, counts):
    keep_mask = aux_map.astype(jnp.bfloat16)
    row_total, aux_total = b_three.shape
    masked = (b_three.reshape(NDB, CW, NAB, AUXW) * keep_mask[:, None, :, None]).reshape(row_total, aux_total)
    fitted = jnp.dot(masked, metric, preferred_element_type=jnp.float32).astype(jnp.bfloat16)
    block_table = fitted.reshape(NDB, CW, aux_total)
    slot_of = jnp.arange(DMAX * CW, dtype=jnp.int32) // CW

    def one_pair(entry):
        block_names, live_count = entry
        stacked = block_table[block_names].reshape(DMAX * CW, aux_total).astype(jnp.float32)
        product = jnp.dot(stacked, stacked.T, preferred_element_type=jnp.float32)
        live_rows = slot_of < live_count
        return jnp.where(live_rows[:, None] & live_rows[None, :], product, jnp.zeros_like(product))

    return lax.map(one_pair, (domains, counts))
```

```python
import functools

import jax
import jax.numpy as jnp
from jax import lax
from jax.experimental import pallas as pl
from jax.experimental.pallas import tpu as pltpu
from jax.sharding import PartitionSpec as P

VMEM_LIMIT = 48 * 1024 * 1024


def mask_kernel(map_ref, b_ref, out_ref):
    blocks_dev, aux_blocks = map_ref.shape
    rows_dev, aux_dev = b_ref.shape
    width = rows_dev // blocks_dev
    aux_width = aux_dev // aux_blocks
    spread = (
        lax.broadcasted_iota(jnp.int32, (aux_blocks, aux_dev), 1) // aux_width
        == lax.broadcasted_iota(jnp.int32, (aux_blocks, aux_dev), 0)
    ).astype(jnp.float32)
    keep = jnp.dot(map_ref[...].astype(jnp.float32), spread, preferred_element_type=jnp.float32)
    keep = keep.astype(jnp.bfloat16)
    for block in range(blocks_dev):
        rows = slice(block * width, (block + 1) * width)
        out_ref[rows, :] = b_ref[rows, :] * keep[block : block + 1, :]


def fit_kernel(blocks_dev, send_ref, m_ref, w_ref, out_ref, total, fitted, sems):
    step = pl.program_id(0)
    steps = pl.num_programs(0)
    slots = out_ref.shape[0]
    part = jnp.dot(m_ref[0], w_ref[...], preferred_element_type=jnp.float32)

    @pl.when(step == 0)
    def _():
        total[...] = part

    @pl.when(step > 0)
    def _():
        total[...] += part

    @pl.when(step == steps - 1)
    def _():
        fitted[...] = total[...].astype(jnp.bfloat16).reshape(fitted.shape)
        copies = [
            pltpu.make_async_copy(fitted.at[send_ref[slot]], out_ref.at[slot], sems.at[slot])
            for slot in range(slots)
        ]
        for copy in copies:
            copy.start()
        for copy in copies:
            copy.wait()


def gram_kernel(where_ref, counts_ref, s0, s1, s2, s3, out_ref):
    pair = pl.program_id(0)
    width = s0.shape[1]
    stack = jnp.concatenate([s0[0], s1[0], s2[0], s3[0]], axis=0)
    size = stack.shape[0]
    value = lax.dot_general(
        stack, stack, (((1,), (1,)), ((), ())), preferred_element_type=jnp.float32
    )
    live = counts_ref[pair] * width
    row = lax.broadcasted_iota(jnp.int32, (size, size), 0)
    column = lax.broadcasted_iota(jnp.int32, (size, size), 1)
    value = jnp.where(jnp.maximum(row, column) < live, value, 0.0)
    out_ref[...] = value.reshape(out_ref.shape)


def per_device(b_three, metric, aux_map, domains, counts):
    rows_dev, aux_dev = b_three.shape
    blocks_dev, _ = aux_map.shape
    width = rows_dev // blocks_dev
    n_pair = lax.axis_size("pair")
    n_aux = lax.axis_size("aux")
    own = lax.axis_index("pair")
    pairs_dev = counts.shape[0]
    domain_max = domains.shape[1]
    slots_dev = pairs_dev * domain_max
    cap = 2

    masked = pl.pallas_call(
        mask_kernel,
        out_shape=jax.ShapeDtypeStruct(b_three.shape, jnp.bfloat16),
        compiler_params=pltpu.CompilerParams(vmem_limit_bytes=VMEM_LIMIT),
        name="mask",
    )(aux_map, b_three)
    gathered = lax.all_gather(masked, "aux", axis=0)

    table = domains.reshape(n_pair, slots_dev)
    owner = table // blocks_dev
    same = owner[:, :, None] == owner[:, None, :]
    earlier = jnp.tril(jnp.ones((slots_dev, slots_dev), jnp.bool_), -1)
    rank = jnp.sum((same & earlier[None]).astype(jnp.int32), axis=2)
    local = table % blocks_dev
    hit = (owner == own)[:, None, :] & (rank[:, None, :] == jnp.arange(cap, dtype=jnp.int32)[None, :, None])
    send = jnp.sum(jnp.where(hit, local[:, None, :], 0), axis=2).reshape(n_pair * cap)
    here = jnp.arange(n_pair, dtype=jnp.int32)[:, None] == own
    where = jnp.sum(jnp.where(here, owner * cap + rank, 0), axis=0)

    slots = n_pair * cap
    picked = pl.pallas_call(
        functools.partial(fit_kernel, blocks_dev),
        grid_spec=pltpu.PrefetchScalarGridSpec(
            num_scalar_prefetch=1,
            grid=(n_aux,),
            in_specs=[
                pl.BlockSpec((1, rows_dev, aux_dev), lambda k, send: (k, 0, 0)),
                pl.BlockSpec((aux_dev, aux_dev), lambda k, send: (k, 0)),
            ],
            out_specs=pl.BlockSpec(memory_space=pl.ANY),
            scratch_shapes=[
                pltpu.VMEM((rows_dev, aux_dev), jnp.float32),
                pltpu.VMEM((blocks_dev, width, aux_dev), jnp.bfloat16),
                pltpu.SemaphoreType.DMA((slots,)),
            ],
        ),
        out_shape=jax.ShapeDtypeStruct((slots, width, aux_dev), jnp.bfloat16),
        compiler_params=pltpu.CompilerParams(vmem_limit_bytes=VMEM_LIMIT),
        name="fit",
    )(send, gathered, metric)

    arrived = lax.all_to_all(
        picked.reshape(n_pair, cap * width, aux_dev), "pair", split_axis=0, concat_axis=0, tiled=True
    ).reshape(slots, width, aux_dev)

    size = domain_max * width
    share = size // n_aux

    def slot_spec(index):
        return pl.BlockSpec(
            (1, width, aux_dev), lambda p, where, live: (where[p * domain_max + index], 0, 0)
        )

    partial_value = pl.pallas_call(
        gram_kernel,
        grid_spec=pltpu.PrefetchScalarGridSpec(
            num_scalar_prefetch=2,
            grid=(pairs_dev,),
            in_specs=[slot_spec(index) for index in range(domain_max)],
            out_specs=pl.BlockSpec((n_aux, 1, share, size), lambda p, where, live: (0, p, 0, 0)),
        ),
        out_shape=jax.ShapeDtypeStruct((n_aux, pairs_dev, share, size), jnp.float32),
        compiler_params=pltpu.CompilerParams(vmem_limit_bytes=VMEM_LIMIT),
        name="gram",
    )(where, counts, arrived, arrived, arrived, arrived)
    return lax.psum_scatter(partial_value, "aux", scatter_dimension=0, tiled=False)


def solution(mesh):
    return jax.shard_map(
        per_device,
        mesh=mesh,
        in_specs=(P("pair", "aux"), P(None, "aux"), P("pair", "aux"), P(), P("pair")),
        out_specs=P("pair", "aux", None),
        check_vma=False,
    )
```

```python
import functools

import jax
import jax.numpy as jnp
from jax import lax
from jax.experimental import pallas as pl
from jax.experimental.pallas import tpu as pltpu
from jax.sharding import PartitionSpec as P

VMEM_LIMIT = 48 * 1024 * 1024
SIDE = 4
CAP = 2


def mask_kernel(map_ref, b_ref, out_ref):
    blocks_dev, aux_blocks = map_ref.shape
    rows_dev, aux_dev = b_ref.shape
    width = rows_dev // blocks_dev
    aux_width = aux_dev // aux_blocks
    spread = (
        lax.broadcasted_iota(jnp.int32, (aux_blocks, aux_dev), 1) // aux_width
        == lax.broadcasted_iota(jnp.int32, (aux_blocks, aux_dev), 0)
    ).astype(jnp.float32)
    keep = jnp.dot(map_ref[...].astype(jnp.float32), spread, preferred_element_type=jnp.float32)
    keep = keep.astype(jnp.bfloat16)
    for block in range(blocks_dev):
        rows = slice(block * width, (block + 1) * width)
        out_ref[rows, :] = b_ref[rows, :] * keep[block : block + 1, :]


def fit_kernel(m_ref, w_ref, out_ref, total):
    step = pl.program_id(0)
    part = jnp.dot(m_ref[0], w_ref[...], preferred_element_type=jnp.float32)

    @pl.when(step == 0)
    def _():
        total[...] = part

    @pl.when(step > 0)
    def _():
        total[...] += part

    @pl.when(step == pl.num_programs(0) - 1)
    def _():
        out_ref[...] = total[...].astype(jnp.bfloat16).reshape(out_ref.shape)


def pick_kernel(send_ref, *refs):
    sources, outs = refs[:SIDE], refs[SIDE : SIDE + 2 * SIDE]
    held, load_sems, store_sems = refs[SIDE + 2 * SIDE :]
    blocks_dev = sources[0].shape[0]
    slots = outs[0].shape[0]
    loads = [
        pltpu.make_async_copy(source, held.at[pl.ds(index * blocks_dev, blocks_dev)], load_sems.at[index])
        for index, source in enumerate(sources)
    ]
    for load in loads:
        load.start()
    for load in loads:
        load.wait()
    stores = [
        pltpu.make_async_copy(
            held.at[send_ref[message * slots + slot]], out.at[slot], store_sems.at[message * slots + slot]
        )
        for message, out in enumerate(outs)
        for slot in range(slots)
    ]
    for store in stores:
        store.start()
    for store in stores:
        store.wait()


def gram_kernel(domain_max, where_ref, counts_ref, *refs):
    messages = 2 * SIDE
    arrived, out_ref = refs[:messages], refs[messages]
    held, values, load_sems, store_sems = refs[messages + 1 :]
    slots = arrived[0].shape[0]
    pairs_dev, n_aux, share, size = values.shape
    width = held.shape[1]
    loads = [
        pltpu.make_async_copy(source, held.at[pl.ds(index * slots, slots)], load_sems.at[index])
        for index, source in enumerate(arrived)
    ]
    for load in loads:
        load.start()
    for load in loads:
        load.wait()
    row = lax.broadcasted_iota(jnp.int32, (size, size), 0)
    column = lax.broadcasted_iota(jnp.int32, (size, size), 1)
    furthest = jnp.maximum(row, column)
    stores = []
    for pair in range(pairs_dev):
        stack = jnp.concatenate(
            [held[where_ref[pair * domain_max + index]] for index in range(domain_max)], axis=0
        )
        value = lax.dot_general(
            stack, stack, (((1,), (1,)), ((), ())), preferred_element_type=jnp.float32
        )
        value = jnp.where(furthest < counts_ref[pair] * width, value, 0.0)
        values[pair] = value.reshape(n_aux, share, size)
        store = pltpu.make_async_copy(values.at[pair], out_ref.at[:, pair], store_sems.at[pair])
        store.start()
        stores.append(store)
    for store in stores:
        store.wait()


def device_of(x, y, core):
    return (x % SIDE) * 2 * SIDE + (y % SIDE) * 2 + core % 2


def gather_perm(hop):
    return [
        (device_of(x, y, core), device_of(x + hop, y, 0) if core == 0 else device_of(x, y + hop, 1))
        for x in range(SIDE)
        for y in range(SIDE)
        for core in range(2)
    ]


def spread_perm(hop, flip):
    return [
        (
            device_of(x, y, core),
            device_of(x, y + hop, flip) if core == 0 else device_of(x + hop, y, 1 - flip),
        )
        for x in range(SIDE)
        for y in range(SIDE)
        for core in range(2)
    ]


def plan(domains, own, pairs_dev, blocks_dev, n_pair):
    table = domains.reshape(n_pair, pairs_dev * domains.shape[1])
    slots_dev = table.shape[1]
    x, y, core = own // (2 * SIDE), (own // 2) % SIDE, own % 2
    first = core == 0
    hops = jnp.arange(SIDE, dtype=jnp.int32)
    flips = jnp.arange(2, dtype=jnp.int32)
    source = jnp.where(first, device_of(x - hops, y, 0), device_of(x, y - hops, 1))
    target = jnp.where(
        first,
        device_of(x, y + hops[:, None], flips[None, :]),
        device_of(x + hops[:, None], y, 1 - flips[None, :]),
    ).reshape(2 * SIDE)

    owner, local = table // blocks_dev, table % blocks_dev
    earlier = jnp.tril(jnp.ones((slots_dev, slots_dev), jnp.bool_), -1)
    rank = jnp.sum(((owner[:, :, None] == owner[:, None, :]) & earlier[None]).astype(jnp.int32), axis=2)

    packed = (owner * CAP + rank) * blocks_dev + local
    chosen = jnp.concatenate([target, own[None]])[:, None] == jnp.arange(n_pair, dtype=jnp.int32)[None, :]
    rows = jnp.sum(jnp.where(chosen[:, :, None], packed[None], 0), axis=1)
    key = rows // blocks_dev
    wanted = (source[:, None] * CAP + jnp.arange(CAP, dtype=jnp.int32)[None, :]).reshape(SIDE * CAP)
    from_hop = (jnp.arange(SIDE * CAP, dtype=jnp.int32) // CAP) * blocks_dev
    hit = key[:-1, None, :] == wanted[None, :, None]
    send = from_hop[None, :] + jnp.sum(jnp.where(hit, rows[:-1, None, :] % blocks_dev, 0), axis=2)

    named, place = key[-1] // CAP, key[-1] % CAP
    back_x, back_y = (x - named // (2 * SIDE)) % SIDE, (y - (named // 2) % SIDE) % SIDE
    sent_first = named % 2 == 0
    gathered = jnp.where(sent_first, back_x, back_y)
    spread = jnp.where(sent_first, back_y, back_x)
    flip = jnp.where(sent_first, core, 1 - core)
    where = ((spread * 2 + flip) * SIDE + gathered) * CAP + place
    return send.reshape(-1), where


def per_device(b_three, metric, aux_map, domains, counts):
    rows_dev, aux_dev = b_three.shape
    blocks_dev, _ = aux_map.shape
    width = rows_dev // blocks_dev
    n_pair = lax.axis_size("pair")
    n_aux = lax.axis_size("aux")
    own = lax.axis_index("pair")
    pairs_dev = counts.shape[0]
    domain_max = domains.shape[1]
    params = pltpu.CompilerParams(vmem_limit_bytes=VMEM_LIMIT)
    anywhere = pl.BlockSpec(memory_space=pl.ANY)

    masked = pl.pallas_call(
        mask_kernel,
        out_shape=jax.ShapeDtypeStruct(b_three.shape, jnp.bfloat16),
        compiler_params=params,
        name="mask",
    )(aux_map, b_three)
    gathered = lax.all_gather(masked, "aux", axis=0)
    send, where = plan(domains, own, pairs_dev, blocks_dev, n_pair)

    block_shape = (width, aux_dev)
    fitted = pl.pallas_call(
        fit_kernel,
        grid=(n_aux,),
        in_specs=[
            pl.BlockSpec((1, rows_dev, aux_dev), lambda k: (k, 0, 0)),
            pl.BlockSpec((aux_dev, aux_dev), lambda k: (k, 0)),
        ],
        out_specs=pl.BlockSpec((blocks_dev, *block_shape), lambda k: (0, 0, 0)),
        scratch_shapes=[pltpu.VMEM((rows_dev, aux_dev), jnp.float32)],
        out_shape=jax.ShapeDtypeStruct((blocks_dev, *block_shape), jnp.bfloat16),
        compiler_params=params,
        name="fit",
    )(gathered, metric)

    sources = {0: fitted}
    for hop in (1, 3, 2):
        sources[hop] = lax.ppermute(fitted, "pair", gather_perm(hop))

    messages, slots = 2 * SIDE, SIDE * CAP
    picked = pl.pallas_call(
        pick_kernel,
        grid_spec=pltpu.PrefetchScalarGridSpec(
            num_scalar_prefetch=1,
            grid=(),
            in_specs=[anywhere] * SIDE,
            out_specs=[anywhere] * messages,
            scratch_shapes=[
                pltpu.VMEM((SIDE * blocks_dev, *block_shape), jnp.bfloat16),
                pltpu.SemaphoreType.DMA((SIDE,)),
                pltpu.SemaphoreType.DMA((messages * slots,)),
            ],
        ),
        out_shape=[jax.ShapeDtypeStruct((slots, *block_shape), jnp.bfloat16)] * messages,
        compiler_params=params,
        name="pick",
    )(send, *[sources[hop] for hop in range(SIDE)])

    arrived = {0: picked[0]}
    for hop, flip in ((1, 0), (3, 0), (1, 1), (3, 1), (2, 0), (2, 1), (0, 1)):
        message = hop * 2 + flip
        arrived[message] = lax.ppermute(picked[message], "pair", spread_perm(hop, flip))

    size = domain_max * width
    share = size // n_aux
    partial_value = pl.pallas_call(
        functools.partial(gram_kernel, domain_max),
        grid_spec=pltpu.PrefetchScalarGridSpec(
            num_scalar_prefetch=2,
            grid=(),
            in_specs=[anywhere] * messages,
            out_specs=anywhere,
            scratch_shapes=[
                pltpu.VMEM((messages * slots, *block_shape), jnp.bfloat16),
                pltpu.VMEM((pairs_dev, n_aux, share, size), jnp.float32),
                pltpu.SemaphoreType.DMA((messages,)),
                pltpu.SemaphoreType.DMA((pairs_dev,)),
            ],
        ),
        out_shape=jax.ShapeDtypeStruct((n_aux, pairs_dev, share, size), jnp.float32),
        compiler_params=params,
        name="gram",
    )(where, counts, *[arrived[message] for message in range(messages)])
    return lax.psum_scatter(partial_value, "aux", scatter_dimension=0, tiled=False)


def solution(mesh):
    return jax.shard_map(
        per_device,
        mesh=mesh,
        in_specs=(P("pair", "aux"), P(None, "aux"), P("pair", "aux"), P(), P("pair")),
        out_specs=P("pair", "aux", None),
        check_vma=False,
    )
```

```python
import functools

import jax
import jax.numpy as jnp
from jax import lax
from jax.experimental import pallas as pl
from jax.experimental.pallas import tpu as pltpu
from jax.sharding import PartitionSpec as P

VMEM_LIMIT = 48 * 1024 * 1024
CHUNKS = (5, 3)
SIDE = 4
CAP = 2


def mask_kernel(map_ref, b_ref, *out_refs):
    blocks_dev, aux_blocks = map_ref.shape
    rows_dev, aux_dev = b_ref.shape
    width = rows_dev // blocks_dev
    aux_width = aux_dev // aux_blocks
    spread = (
        lax.broadcasted_iota(jnp.int32, (aux_blocks, aux_dev), 1) // aux_width
        == lax.broadcasted_iota(jnp.int32, (aux_blocks, aux_dev), 0)
    ).astype(jnp.float32)
    keep = jnp.dot(map_ref[...].astype(jnp.float32), spread, preferred_element_type=jnp.float32)
    keep = keep.astype(jnp.bfloat16)
    block = 0
    for out_ref in out_refs:
        for start in range(0, out_ref.shape[0], width):
            out_ref[start : start + width, :] = (
                b_ref[block * width : (block + 1) * width, :] * keep[block : block + 1, :]
            )
            block += 1


def fit_kernel(hops, own_ref, *refs):
    steps = len(hops)
    pieces, w_ref, out_ref = refs[:steps], refs[steps], refs[steps + 1]
    left, right, total, left_sems, right_sems = refs[steps + 2 :]
    depth = right.shape[1]
    loads = []
    for step, hop in enumerate(hops):
        row = pl.multiple_of(((own_ref[0] + steps - hop) % steps) * depth, depth)
        loads.append(
            (
                pltpu.make_async_copy(pieces[step], left.at[step], left_sems.at[step]),
                pltpu.make_async_copy(w_ref.at[pl.ds(row, depth)], right.at[step], right_sems.at[step]),
            )
        )
    for pair in loads:
        for load in pair:
            load.start()

    total[...] = jnp.zeros_like(total)

    @pl.loop(0, steps)
    def _(step):
        pltpu.make_async_copy(pieces[0], left.at[step], left_sems.at[step]).wait()
        pltpu.make_async_copy(w_ref.at[pl.ds(0, depth)], right.at[step], right_sems.at[step]).wait()
        total[...] += jnp.dot(left[step], right[step], preferred_element_type=jnp.float32)

    out_ref[...] = total[...].astype(jnp.bfloat16).reshape(out_ref.shape)


def pick_kernel(send_ref, *refs):
    count = SIDE * len(CHUNKS)
    sources, outs = refs[:count], refs[count : count + 2 * SIDE]
    held, load_sems, store_sems = refs[count + 2 * SIDE :]
    slots = outs[0].shape[0]
    loads, block = [], 0
    for index, source in enumerate(sources):
        loads.append(
            pltpu.make_async_copy(source, held.at[pl.ds(block, source.shape[0])], load_sems.at[index])
        )
        block += source.shape[0]
    for load in loads:
        load.start()
    for load in loads:
        load.wait()
    stores = [
        pltpu.make_async_copy(
            held.at[send_ref[message * slots + slot]], out.at[slot], store_sems.at[message * slots + slot]
        )
        for message, out in enumerate(outs)
        for slot in range(slots)
    ]
    for store in stores:
        store.start()
    for store in stores:
        store.wait()


def gram_kernel(domain_max, where_ref, counts_ref, own_ref, *refs):
    messages = 2 * SIDE
    arrived, out_refs = refs[:messages], refs[messages : messages + 2]
    held, values, load_sems, store_sems = refs[messages + 2 :]
    slots = arrived[0].shape[0]
    n_aux, pairs_dev, share, size = values.shape
    width = held.shape[1]
    half = out_refs[0].shape[1]
    loads = [
        pltpu.make_async_copy(source, held.at[pl.ds(index * slots, slots)], load_sems.at[index])
        for index, source in enumerate(arrived)
    ]
    for load in loads:
        load.start()
    for load in loads:
        load.wait()
    row = lax.broadcasted_iota(jnp.int32, (size, size), 0)
    column = lax.broadcasted_iota(jnp.int32, (size, size), 1)
    furthest = jnp.maximum(row, column)
    stores = []
    for index, out in enumerate(out_refs):

        @pl.loop(index * half, (index + 1) * half)
        def _(pair):
            stack = jnp.concatenate(
                [held[where_ref[pair * domain_max + index]] for index in range(domain_max)], axis=0
            )
            value = lax.dot_general(
                stack, stack, (((1,), (1,)), ((), ())), preferred_element_type=jnp.float32
            )
            value = jnp.where(furthest < counts_ref[pair] * width, value, 0.0)
            value = value.reshape(n_aux, share, size)
            for index in range(n_aux):
                values[(index + n_aux - own_ref[0]) % n_aux, pair] = value[index]

        store = pltpu.make_async_copy(
            values.at[:, pl.ds(index * half, half)], out, store_sems.at[index]
        )
        store.start()
        stores.append(store)
    for store in stores:
        store.wait()


def ring_gather(chunks):
    n_aux = lax.axis_size("aux")
    rings = []
    for index, chunk in enumerate(chunks):
        far = n_aux // 2 if index % 2 == 0 else n_aux // 2 - 1
        rings.append((far, n_aux - 1 - far, {0: chunk}, [chunk, chunk]))
    for step in range(1, n_aux // 2 + 1):
        for far_right, far_left, found, moving in rings:
            if step <= far_right:
                moving[0] = shift(moving[0], 1)
                found[step] = moving[0]
            if step <= far_left:
                moving[1] = shift(moving[1], -1)
                found[n_aux - step] = moving[1]
    return [found for _, _, found, _ in rings]


def ring_sum(parts):
    n_aux = lax.axis_size("aux")
    rings = []
    for index, part in enumerate(parts):
        far = n_aux // 2 if index % 2 == 0 else n_aux // 2 - 1
        rings.append([part, far, n_aux - 1 - far, None, None])
    for step in range(n_aux // 2, 0, -1):
        for ring in rings:
            part, far_right, far_left, right, left = ring
            if step <= far_right:
                ring[3] = shift(part[step] if right is None else right + part[step], 1)
            if step <= far_left:
                ring[4] = shift(part[n_aux - step] if left is None else left + part[n_aux - step], -1)
    return [part[0] + right + left for part, _, _, right, left in rings]


def shift(value, by):
    n_aux = lax.axis_size("aux")
    return lax.ppermute(value, "aux", [(index, (index + by) % n_aux) for index in range(n_aux)])


def device_of(x, y, core):
    return (x % SIDE) * 2 * SIDE + (y % SIDE) * 2 + core % 2


def gather_perm(hop):
    return [
        (device_of(x, y, core), device_of(x + hop, y, 0) if core == 0 else device_of(x, y + hop, 1))
        for x in range(SIDE)
        for y in range(SIDE)
        for core in range(2)
    ]


def spread_perm(hop, flip):
    return [
        (
            device_of(x, y, core),
            device_of(x, y + hop, flip) if core == 0 else device_of(x + hop, y, 1 - flip),
        )
        for x in range(SIDE)
        for y in range(SIDE)
        for core in range(2)
    ]


def plan(domains, own, pairs_dev, blocks_dev, n_pair):
    table = domains.reshape(n_pair, pairs_dev * domains.shape[1])
    slots_dev = table.shape[1]
    x, y, core = own // (2 * SIDE), (own // 2) % SIDE, own % 2
    first = core == 0
    hops = jnp.arange(SIDE, dtype=jnp.int32)
    flips = jnp.arange(2, dtype=jnp.int32)
    source = jnp.where(first, device_of(x - hops, y, 0), device_of(x, y - hops, 1))
    target = jnp.where(
        first,
        device_of(x, y + hops[:, None], flips[None, :]),
        device_of(x + hops[:, None], y, 1 - flips[None, :]),
    ).reshape(2 * SIDE)

    owner, local = table // blocks_dev, table % blocks_dev
    earlier = jnp.tril(jnp.ones((slots_dev, slots_dev), jnp.bool_), -1)
    rank = jnp.sum(((owner[:, :, None] == owner[:, None, :]) & earlier[None]).astype(jnp.int32), axis=2)

    packed = (owner * CAP + rank) * blocks_dev + local
    chosen = jnp.concatenate([target, own[None]])[:, None] == jnp.arange(n_pair, dtype=jnp.int32)[None, :]
    rows = jnp.sum(jnp.where(chosen[:, :, None], packed[None], 0), axis=1)
    key = rows // blocks_dev
    wanted = (source[:, None] * CAP + jnp.arange(CAP, dtype=jnp.int32)[None, :]).reshape(SIDE * CAP)
    from_hop = (jnp.arange(SIDE * CAP, dtype=jnp.int32) // CAP) * blocks_dev
    hit = key[:-1, None, :] == wanted[None, :, None]
    send = from_hop[None, :] + jnp.sum(jnp.where(hit, rows[:-1, None, :] % blocks_dev, 0), axis=2)

    named, place = key[-1] // CAP, key[-1] % CAP
    back_x, back_y = (x - named // (2 * SIDE)) % SIDE, (y - (named // 2) % SIDE) % SIDE
    sent_first = named % 2 == 0
    gathered = jnp.where(sent_first, back_x, back_y)
    spread = jnp.where(sent_first, back_y, back_x)
    flip = jnp.where(sent_first, core, 1 - core)
    where = ((spread * 2 + flip) * SIDE + gathered) * CAP + place
    return send.reshape(-1), where


def per_device(b_three, metric, aux_map, domains, counts):
    rows_dev, aux_dev = b_three.shape
    blocks_dev, _ = aux_map.shape
    width = rows_dev // blocks_dev
    n_pair = lax.axis_size("pair")
    n_aux = lax.axis_size("aux")
    own = lax.axis_index("pair")
    pairs_dev = counts.shape[0]
    domain_max = domains.shape[1]
    params = pltpu.CompilerParams(vmem_limit_bytes=VMEM_LIMIT)
    anywhere = pl.BlockSpec(memory_space=pl.ANY)

    place = lax.axis_index("aux").astype(jnp.int32).reshape(1)

    masked = pl.pallas_call(
        mask_kernel,
        out_shape=[jax.ShapeDtypeStruct((blocks * width, aux_dev), jnp.bfloat16) for blocks in CHUNKS],
        compiler_params=params,
        name="mask",
    )(aux_map, b_three)
    rings = ring_gather(masked)
    send, where = plan(domains, own, pairs_dev, blocks_dev, n_pair)

    block_shape = (width, aux_dev)
    sources = {}
    for index, (blocks, ring) in enumerate(zip(CHUNKS, rings)):
        hops = tuple(ring)
        fitted = pl.pallas_call(
            functools.partial(fit_kernel, hops),
            grid_spec=pltpu.PrefetchScalarGridSpec(
                num_scalar_prefetch=1,
                grid=(),
                in_specs=[anywhere] * (n_aux + 1),
                out_specs=pl.BlockSpec(memory_space=pltpu.VMEM),
                scratch_shapes=[
                    pltpu.VMEM((n_aux, blocks * width, aux_dev), jnp.bfloat16),
                    pltpu.VMEM((n_aux, aux_dev, aux_dev), jnp.bfloat16),
                    pltpu.VMEM((blocks * width, aux_dev), jnp.float32),
                    pltpu.SemaphoreType.DMA((n_aux,)),
                    pltpu.SemaphoreType.DMA((n_aux,)),
                ],
            ),
            out_shape=jax.ShapeDtypeStruct((blocks, *block_shape), jnp.bfloat16),
            compiler_params=params,
            name="fit",
        )(place, *[ring[hop] for hop in hops], metric)
        sources[0, index] = fitted
        for hop in (1, 3, 2):
            sources[hop, index] = lax.ppermute(fitted, "pair", gather_perm(hop))

    messages, slots = 2 * SIDE, SIDE * CAP
    picked = pl.pallas_call(
        pick_kernel,
        grid_spec=pltpu.PrefetchScalarGridSpec(
            num_scalar_prefetch=1,
            grid=(),
            in_specs=[anywhere] * (SIDE * len(CHUNKS)),
            out_specs=[anywhere] * messages,
            scratch_shapes=[
                pltpu.VMEM((SIDE * blocks_dev, *block_shape), jnp.bfloat16),
                pltpu.SemaphoreType.DMA((SIDE * len(CHUNKS),)),
                pltpu.SemaphoreType.DMA((messages * slots,)),
            ],
        ),
        out_shape=[jax.ShapeDtypeStruct((slots, *block_shape), jnp.bfloat16)] * messages,
        compiler_params=params,
        name="pick",
    )(send, *[sources[hop, index] for hop in range(SIDE) for index in range(len(CHUNKS))])

    arrived = {0: picked[0]}
    for hop, flip in ((1, 0), (3, 0), (1, 1), (3, 1), (2, 0), (2, 1), (0, 1)):
        message = hop * 2 + flip
        arrived[message] = lax.ppermute(picked[message], "pair", spread_perm(hop, flip))

    size = domain_max * width
    share = size // n_aux
    half = pairs_dev // 2
    partial_values = pl.pallas_call(
        functools.partial(gram_kernel, domain_max),
        grid_spec=pltpu.PrefetchScalarGridSpec(
            num_scalar_prefetch=3,
            grid=(),
            in_specs=[anywhere] * messages,
            out_specs=[anywhere] * 2,
            scratch_shapes=[
                pltpu.VMEM((messages * slots, *block_shape), jnp.bfloat16),
                pltpu.VMEM((n_aux, pairs_dev, share, size), jnp.float32),
                pltpu.SemaphoreType.DMA((messages,)),
                pltpu.SemaphoreType.DMA((2,)),
            ],
        ),
        out_shape=[jax.ShapeDtypeStruct((n_aux, half, share, size), jnp.float32)] * 2,
        compiler_params=params,
        name="gram",
    )(where, counts, place, *[arrived[message] for message in range(messages)])
    return jnp.concatenate(ring_sum(partial_values), axis=0)


def solution(mesh):
    return jax.shard_map(
        per_device,
        mesh=mesh,
        in_specs=(P("pair", "aux"), P(None, "aux"), P("pair", "aux"), P(), P("pair")),
        out_specs=P("pair", "aux", None),
        check_vma=False,
    )
```

```python
import functools

import jax
import jax.numpy as jnp
from jax import lax
from jax.experimental import pallas as pl
from jax.experimental.pallas import tpu as pltpu
from jax.sharding import PartitionSpec as P

VMEM_LIMIT = 16 * 1024 * 1024
CHUNKS = (5, 3)
SIDE = 4
CAP = 2


def mask_kernel(map_ref, b_ref, *out_refs):
    blocks_dev, aux_blocks = map_ref.shape
    rows_dev, aux_dev = b_ref.shape
    width = rows_dev // blocks_dev
    aux_width = aux_dev // aux_blocks
    spread = (
        lax.broadcasted_iota(jnp.int32, (aux_blocks, aux_dev), 1) // aux_width
        == lax.broadcasted_iota(jnp.int32, (aux_blocks, aux_dev), 0)
    ).astype(jnp.float32)
    keep = jnp.dot(map_ref[...].astype(jnp.float32), spread, preferred_element_type=jnp.float32)
    keep = keep.astype(jnp.bfloat16)
    block = 0
    for out_ref in out_refs:
        for start in range(0, out_ref.shape[0], width):
            out_ref[start : start + width, :] = (
                b_ref[block * width : (block + 1) * width, :] * keep[block : block + 1, :]
            )
            block += 1


def metric_kernel(hops, own_ref, w_ref, out_ref, sems):
    steps = len(hops)
    depth = out_ref.shape[1]
    loads = []
    for step, hop in enumerate(hops):
        row = pl.multiple_of(((own_ref[0] + steps - hop) % steps) * depth, depth)
        loads.append(pltpu.make_async_copy(w_ref.at[pl.ds(row, depth)], out_ref.at[step], sems.at[step]))
    for load in loads:
        load.start()
    for load in loads:
        load.wait()


def fit_kernel(*refs):
    pieces, w_ref, out_ref, total = refs[:-3], refs[-3], refs[-2], refs[-1]
    for step, piece in enumerate(pieces):
        part = jnp.dot(piece[...], w_ref[step], preferred_element_type=jnp.float32)
        if step == 0:
            total[...] = part
        elif step < len(pieces) - 1:
            total[...] += part
        else:
            out_ref[...] = (total[...] + part).astype(jnp.bfloat16).reshape(out_ref.shape)


def pick_kernel(send_ref, *refs):
    count = SIDE * len(CHUNKS)
    sources, outs = refs[:count], refs[count:]
    slots = outs[0].shape[0]
    for message, out in enumerate(outs):
        for slot in range(slots):
            block = send_ref[message * slots + slot]
            start = 0
            for chunk, blocks in enumerate(CHUNKS):
                source = sources[(slot // CAP) * len(CHUNKS) + chunk]

                @pl.when((block >= start) & (block < start + blocks))
                def _(out=out, slot=slot, source=source, index=block - start):
                    out[slot] = source[index]

                start += blocks


def gram_kernel(first_pair, domain_max, goes_ref, counts_ref, own_ref, *refs):
    arrived, out_ref, stacks = refs[:-2], refs[-2], refs[-1]
    slots = arrived[0].shape[0]
    n_aux, pairs, share, size = out_ref.shape
    places, width, depth = stacks.shape
    for message, source in enumerate(arrived):
        for slot in range(slots):
            goes = goes_ref[message * slots + slot] - first_pair * domain_max

            @pl.when((goes >= 0) & (goes < places))
            def _(source=source, slot=slot, goes=goes):
                stacks[goes] = source[slot]

    row = lax.broadcasted_iota(jnp.int32, (size, size), 0)
    column = lax.broadcasted_iota(jnp.int32, (size, size), 1)
    furthest = jnp.maximum(row, column)
    for pair in range(pairs):
        stack = stacks[pair * domain_max : (pair + 1) * domain_max].reshape(size, depth)
        value = lax.dot_general(
            stack, stack, (((1,), (1,)), ((), ())), preferred_element_type=jnp.float32
        )
        value = jnp.where(furthest < counts_ref[first_pair + pair] * width, value, 0.0)
        value = value.reshape(n_aux, share, size)
        for index in range(n_aux):
            out_ref[(index + n_aux - own_ref[0]) % n_aux, pair] = value[index]


def ring_gather(chunks):
    n_aux = lax.axis_size("aux")
    rings = []
    for index, chunk in enumerate(chunks):
        far = n_aux // 2 if index % 2 == 0 else n_aux // 2 - 1
        rings.append((far, n_aux - 1 - far, {0: chunk}, [chunk, chunk]))
    for step in range(1, n_aux // 2 + 1):
        for far_right, far_left, found, moving in rings:
            if step <= far_right:
                moving[0] = shift(moving[0], 1)
                found[step] = moving[0]
            if step <= far_left:
                moving[1] = shift(moving[1], -1)
                found[n_aux - step] = moving[1]
    return [found for _, _, found, _ in rings]


def ring_sum(parts):
    n_aux = lax.axis_size("aux")
    rings = []
    for index, part in enumerate(parts):
        far = n_aux // 2 if index % 2 == 0 else n_aux // 2 - 1
        rings.append([part, far, n_aux - 1 - far, None, None])
    for step in range(n_aux // 2, 0, -1):
        for ring in rings:
            part, far_right, far_left, right, left = ring
            if step <= far_right:
                ring[3] = shift(part[step] if right is None else right + part[step], 1)
            if step <= far_left:
                ring[4] = shift(part[n_aux - step] if left is None else left + part[n_aux - step], -1)
    return [part[0] + right + left for part, _, _, right, left in rings]


def shift(value, by):
    n_aux = lax.axis_size("aux")
    return lax.ppermute(value, "aux", [(index, (index + by) % n_aux) for index in range(n_aux)])


def device_of(x, y, core):
    return (x % SIDE) * 2 * SIDE + (y % SIDE) * 2 + core % 2


def gather_perm(hop):
    return [
        (device_of(x, y, core), device_of(x + hop, y, 0) if core == 0 else device_of(x, y + hop, 1))
        for x in range(SIDE)
        for y in range(SIDE)
        for core in range(2)
    ]


def spread_perm(hop, flip):
    return [
        (
            device_of(x, y, core),
            device_of(x, y + hop, flip) if core == 0 else device_of(x + hop, y, 1 - flip),
        )
        for x in range(SIDE)
        for y in range(SIDE)
        for core in range(2)
    ]


def plan(domains, own, pairs_dev, blocks_dev, n_pair):
    table = domains.reshape(n_pair, pairs_dev * domains.shape[1])
    slots_dev = table.shape[1]
    x, y, core = own // (2 * SIDE), (own // 2) % SIDE, own % 2
    first = core == 0
    hops = jnp.arange(SIDE, dtype=jnp.int32)
    flips = jnp.arange(2, dtype=jnp.int32)
    source = jnp.where(first, device_of(x - hops, y, 0), device_of(x, y - hops, 1))
    target = jnp.where(
        first,
        device_of(x, y + hops[:, None], flips[None, :]),
        device_of(x + hops[:, None], y, 1 - flips[None, :]),
    ).reshape(2 * SIDE)

    owner, local = table // blocks_dev, table % blocks_dev
    earlier = jnp.tril(jnp.ones((slots_dev, slots_dev), jnp.bool_), -1)
    rank = jnp.sum(((owner[:, :, None] == owner[:, None, :]) & earlier[None]).astype(jnp.int32), axis=2)

    packed = (owner * CAP + rank) * blocks_dev + local
    chosen = jnp.concatenate([target, own[None]])[:, None] == jnp.arange(n_pair, dtype=jnp.int32)[None, :]
    rows = jnp.sum(jnp.where(chosen[:, :, None], packed[None], 0), axis=1)
    key = rows // blocks_dev
    wanted = (source[:, None] * CAP + jnp.arange(CAP, dtype=jnp.int32)[None, :]).reshape(SIDE * CAP)
    hit = key[:-1, None, :] == wanted[None, :, None]
    send = jnp.sum(jnp.where(hit, rows[:-1, None, :] % blocks_dev, 0), axis=2)

    named, place = key[-1] // CAP, key[-1] % CAP
    back_x, back_y = (x - named // (2 * SIDE)) % SIDE, (y - (named // 2) % SIDE) % SIDE
    sent_first = named % 2 == 0
    gathered = jnp.where(sent_first, back_x, back_y)
    spread = jnp.where(sent_first, back_y, back_x)
    flip = jnp.where(sent_first, core, 1 - core)
    where = ((spread * 2 + flip) * SIDE + gathered) * CAP + place
    arrives = where[None, :] == jnp.arange(2 * SIDE * SIDE * CAP, dtype=jnp.int32)[:, None]
    goes = jnp.sum(jnp.where(arrives, 1 + jnp.arange(slots_dev, dtype=jnp.int32)[None, :], 0), axis=1) - 1
    return send.reshape(-1), goes


def per_device(b_three, metric, aux_map, domains, counts):
    rows_dev, aux_dev = b_three.shape
    blocks_dev, _ = aux_map.shape
    width = rows_dev // blocks_dev
    n_pair = lax.axis_size("pair")
    n_aux = lax.axis_size("aux")
    own = lax.axis_index("pair")
    pairs_dev = counts.shape[0]
    domain_max = domains.shape[1]
    params = pltpu.CompilerParams(vmem_limit_bytes=VMEM_LIMIT)
    anywhere = pl.BlockSpec(memory_space=pl.ANY)

    place = lax.axis_index("aux").astype(jnp.int32).reshape(1)

    masked = pl.pallas_call(
        mask_kernel,
        out_shape=[jax.ShapeDtypeStruct((blocks * width, aux_dev), jnp.bfloat16) for blocks in CHUNKS],
        compiler_params=params,
        name="mask",
    )(aux_map, b_three)
    rings = ring_gather(masked)
    send, goes = plan(domains, own, pairs_dev, blocks_dev, n_pair)

    block_shape = (width, aux_dev)
    in_vmem = pl.BlockSpec(memory_space=pltpu.VMEM)
    orders = tuple(range(n_aux))
    ordered = pl.pallas_call(
        functools.partial(metric_kernel, orders),
        grid_spec=pltpu.PrefetchScalarGridSpec(
            num_scalar_prefetch=1,
            grid=(),
            in_specs=[anywhere],
            out_specs=in_vmem,
            scratch_shapes=[pltpu.SemaphoreType.DMA((n_aux,))],
        ),
        out_shape=jax.ShapeDtypeStruct((n_aux, aux_dev, aux_dev), jnp.bfloat16),
        compiler_params=params,
        name="order_metric",
    )(place, metric)
    sources = {}
    for index, (blocks, ring) in enumerate(zip(CHUNKS, rings)):
        fitted = pl.pallas_call(
            fit_kernel,
            in_specs=[in_vmem] * (n_aux + 1),
            out_specs=in_vmem,
            scratch_shapes=[pltpu.VMEM((blocks * width, aux_dev), jnp.float32)],
            out_shape=jax.ShapeDtypeStruct((blocks, *block_shape), jnp.bfloat16),
            compiler_params=params,
            name="fit",
        )(*[ring[hop] for hop in orders], ordered)
        sources[0, index] = fitted
        for hop in (1, 3, 2):
            sources[hop, index] = lax.ppermute(fitted, "pair", gather_perm(hop))

    messages, slots = 2 * SIDE, SIDE * CAP
    picked = pl.pallas_call(
        pick_kernel,
        grid_spec=pltpu.PrefetchScalarGridSpec(
            num_scalar_prefetch=1,
            grid=(),
            in_specs=[in_vmem] * (SIDE * len(CHUNKS)),
            out_specs=[in_vmem] * messages,
        ),
        out_shape=[jax.ShapeDtypeStruct((slots, *block_shape), jnp.bfloat16)] * messages,
        compiler_params=params,
        name="pick",
    )(send, *[sources[hop, index] for hop in range(SIDE) for index in range(len(CHUNKS))])

    arrived = {0: picked[0]}
    for hop, flip in ((1, 0), (3, 0), (1, 1), (3, 1), (2, 0), (2, 1), (0, 1)):
        message = hop * 2 + flip
        arrived[message] = lax.ppermute(picked[message], "pair", spread_perm(hop, flip))

    size = domain_max * width
    share = size // n_aux
    half = pairs_dev // 2
    partial_values = [
        pl.pallas_call(
            functools.partial(gram_kernel, first_pair, domain_max),
            grid_spec=pltpu.PrefetchScalarGridSpec(
                num_scalar_prefetch=3,
                grid=(),
                in_specs=[in_vmem] * messages,
                out_specs=in_vmem,
                scratch_shapes=[pltpu.VMEM((half * domain_max, *block_shape), jnp.bfloat16)],
            ),
            out_shape=jax.ShapeDtypeStruct((n_aux, half, share, size), jnp.float32),
            compiler_params=params,
            name="gram",
        )(goes, counts, place, *[arrived[message] for message in range(messages)])
        for first_pair in (0, half)
    ]
    return jnp.concatenate(ring_sum(partial_values), axis=0)


def solution(mesh):
    return jax.shard_map(
        per_device,
        mesh=mesh,
        in_specs=(P("pair", "aux"), P(None, "aux"), P("pair", "aux"), P(), P("pair")),
        out_specs=P("pair", "aux", None),
        check_vma=False,
    )
```

```python
import functools

import jax
import jax.numpy as jnp
from jax import lax
from jax.experimental import pallas as pl
from jax.experimental.pallas import tpu as pltpu
from jax.sharding import PartitionSpec as P

VMEM_LIMIT = 12 * 1024 * 1024
CHUNKS = (5, 3)
SIDE = 4
GATHER_HOPS = (1, 3, 2, 0)
SPREAD_ORDER = ((1, 0), (3, 0), (2, 0), (1, 1), (3, 1), (2, 1), (0, 1), (0, 0))
PICK_GROUP = 2
CAP = 2


def mask_kernel(map_hbm, b_hbm, *refs):
    out_refs, map_ref, b_ref, sems = refs[:-3], refs[-3], refs[-2], refs[-1]
    load_map = pltpu.make_async_copy(map_hbm, map_ref, sems.at[0])
    load_b = pltpu.make_async_copy(b_hbm, b_ref, sems.at[1])
    load_map.start()
    load_b.start()
    load_map.wait()
    blocks_dev, aux_blocks = map_ref.shape
    rows_dev, aux_dev = b_ref.shape
    width = rows_dev // blocks_dev
    aux_width = aux_dev // aux_blocks
    spread = (
        lax.broadcasted_iota(jnp.int32, (aux_blocks, aux_dev), 1) // aux_width
        == lax.broadcasted_iota(jnp.int32, (aux_blocks, aux_dev), 0)
    ).astype(jnp.float32)
    keep = jnp.dot(map_ref[...].astype(jnp.float32), spread, preferred_element_type=jnp.float32)
    keep = keep.astype(jnp.bfloat16)
    load_b.wait()
    block = 0
    for out_ref in out_refs:
        for start in range(0, out_ref.shape[0], width):
            out_ref[start : start + width, :] = (
                b_ref[block * width : (block + 1) * width, :] * keep[block : block + 1, :]
            )
            block += 1


def metric_kernel(hops, own_ref, w_ref, out_ref, sems):
    steps = len(hops)
    depth = out_ref.shape[1]
    loads = []
    for step, hop in enumerate(hops):
        row = pl.multiple_of(((own_ref[0] + steps - hop) % steps) * depth, depth)
        loads.append(pltpu.make_async_copy(w_ref.at[pl.ds(row, depth)], out_ref.at[step], sems.at[step]))
    for load in loads:
        load.start()
    for load in loads:
        load.wait()


def fit_kernel(hops, begun, *refs):
    out_ref, total = refs[-2:]
    start_ref = refs[0] if begun else None
    pieces, w_ref = refs[int(begun) : -3], refs[-3]
    row = 0
    for chunk in range(len(pieces) // len(hops)):
        rows = pieces[chunk * len(hops)].shape[0]
        part = start_ref[row : row + rows, :] if begun else None
        for step, hop in enumerate(hops):
            term = jnp.dot(
                pieces[chunk * len(hops) + step][...], w_ref[hop], preferred_element_type=jnp.float32
            )
            if part is None:
                part = term
            elif step == 0:
                part = part + term
            else:
                part = total[:rows, :] + term
            if step < len(hops) - 1:
                total[:rows, :] = part
        if begun:
            width = out_ref.shape[1]
            out_ref[row // width : (row + rows) // width] = part.astype(jnp.bfloat16).reshape(
                rows // width, width, part.shape[1]
            )
        else:
            out_ref[row : row + rows, :] = part
        row += rows


def pick_kernel(messages, send_ref, *refs):
    sources, outs = refs[:SIDE], refs[SIDE:]
    hop_of = {hop: index for index, hop in enumerate(GATHER_HOPS)}
    for message, out in zip(messages, outs):
        slots = out.shape[0]
        for slot in range(slots):
            out[slot] = sources[hop_of[slot // CAP]][send_ref[message * slots + slot]]


def add_kernel(index, a_ref, part_ref, out_ref):
    out_ref[...] = a_ref[...] + part_ref[index]


def gram_kernel(first_pair, domain_max, order, goes_ref, counts_ref, own_ref, *refs):
    arrived, out_ref, stacks = refs[:-2], refs[-2], refs[-1]
    slots = arrived[0].shape[0]
    n_aux, pairs, share, size = out_ref.shape
    places, width, depth = stacks.shape
    for message, source in zip(order, arrived):
        for slot in range(slots):
            goes = goes_ref[message * slots + slot] - first_pair * domain_max

            @pl.when((goes >= 0) & (goes < places))
            def _(source=source, slot=slot, goes=goes):
                stacks[goes] = source[slot]

    row = lax.broadcasted_iota(jnp.int32, (size, size), 0)
    column = lax.broadcasted_iota(jnp.int32, (size, size), 1)
    furthest = jnp.maximum(row, column)
    for pair in range(pairs):
        stack = stacks[pair * domain_max : (pair + 1) * domain_max].reshape(size, depth)
        value = lax.dot_general(
            stack, stack, (((1,), (1,)), ((), ())), preferred_element_type=jnp.float32
        )
        value = jnp.where(furthest < counts_ref[first_pair + pair] * width, value, 0.0)
        value = value.reshape(n_aux, share, size)
        for index in range(n_aux):
            out_ref[(index + n_aux - own_ref[0]) % n_aux, pair] = value[index]


def ring_gather(chunks):
    n_aux = lax.axis_size("aux")
    rings = []
    for index, chunk in enumerate(chunks):
        far = n_aux // 2 if index % 2 == 0 else n_aux // 2 - 1
        rings.append((far, n_aux - 1 - far, {0: chunk}, [chunk, chunk]))
    for step in range(1, n_aux // 2 + 1):
        for far_right, far_left, found, moving in rings:
            if step <= far_right:
                moving[0] = shift(moving[0], 1)
                found[step] = moving[0]
            if step <= far_left:
                moving[1] = shift(moving[1], -1)
                found[n_aux - step] = moving[1]
    return [found for _, _, found, _ in rings]


def ring_sum(parts):
    n_aux = lax.axis_size("aux")
    rings = []
    for index, part in enumerate(parts):
        far = n_aux // 2 if index % 2 == 0 else n_aux // 2 - 1
        rings.append([part, far, n_aux - 1 - far, None, None])
    for step in range(n_aux // 2, 0, -1):
        for ring in rings:
            part, far_right, far_left, right, left = ring
            if step <= far_right:
                ring[3] = shift(part[step] if right is None else add_term(right, part, step), 1)
            if step <= far_left:
                ring[4] = shift(part[n_aux - step] if left is None else add_term(left, part, n_aux - step), -1)
    return [part[0] + right + left for part, _, _, right, left in rings]


def add_term(moving, part, index):
    in_vmem = pl.BlockSpec(memory_space=pltpu.VMEM)
    return pl.pallas_call(
        functools.partial(add_kernel, index),
        in_specs=[in_vmem] * 2,
        out_specs=in_vmem,
        out_shape=jax.ShapeDtypeStruct(moving.shape, moving.dtype),
        compiler_params=pltpu.CompilerParams(vmem_limit_bytes=VMEM_LIMIT),
        name="add_term",
    )(moving, part)


def shift(value, by):
    n_aux = lax.axis_size("aux")
    return lax.ppermute(value, "aux", [(index, (index + by) % n_aux) for index in range(n_aux)])


def device_of(x, y, core):
    return (x % SIDE) * 2 * SIDE + (y % SIDE) * 2 + core % 2


def gather_perm(hop):
    return [
        (device_of(x, y, core), device_of(x + hop, y, 0) if core == 0 else device_of(x, y + hop, 1))
        for x in range(SIDE)
        for y in range(SIDE)
        for core in range(2)
    ]


def spread_perm(hop, flip):
    return [
        (
            device_of(x, y, core),
            device_of(x, y + hop, flip) if core == 0 else device_of(x + hop, y, 1 - flip),
        )
        for x in range(SIDE)
        for y in range(SIDE)
        for core in range(2)
    ]


def plan(domains, own, pairs_dev, blocks_dev, n_pair):
    table = domains.reshape(n_pair, pairs_dev * domains.shape[1])
    slots_dev = table.shape[1]
    x, y, core = own // (2 * SIDE), (own // 2) % SIDE, own % 2
    first = core == 0
    hops = jnp.arange(SIDE, dtype=jnp.int32)
    flips = jnp.arange(2, dtype=jnp.int32)
    source = jnp.where(first, device_of(x - hops, y, 0), device_of(x, y - hops, 1))
    target = jnp.where(
        first,
        device_of(x, y + hops[:, None], flips[None, :]),
        device_of(x + hops[:, None], y, 1 - flips[None, :]),
    ).reshape(2 * SIDE)

    owner, local = table // blocks_dev, table % blocks_dev
    earlier = jnp.tril(jnp.ones((slots_dev, slots_dev), jnp.bool_), -1)
    rank = jnp.sum(((owner[:, :, None] == owner[:, None, :]) & earlier[None]).astype(jnp.int32), axis=2)

    packed = (owner * CAP + rank) * blocks_dev + local
    chosen = jnp.concatenate([target, own[None]])[:, None] == jnp.arange(n_pair, dtype=jnp.int32)[None, :]
    rows = jnp.sum(jnp.where(chosen[:, :, None], packed[None], 0), axis=1)
    key = rows // blocks_dev
    wanted = (source[:, None] * CAP + jnp.arange(CAP, dtype=jnp.int32)[None, :]).reshape(SIDE * CAP)
    hit = key[:-1, None, :] == wanted[None, :, None]
    send = jnp.sum(jnp.where(hit, rows[:-1, None, :] % blocks_dev, 0), axis=2)

    named, place = key[-1] // CAP, key[-1] % CAP
    back_x, back_y = (x - named // (2 * SIDE)) % SIDE, (y - (named // 2) % SIDE) % SIDE
    sent_first = named % 2 == 0
    gathered = jnp.where(sent_first, back_x, back_y)
    spread = jnp.where(sent_first, back_y, back_x)
    flip = jnp.where(sent_first, core, 1 - core)
    where = ((spread * 2 + flip) * SIDE + gathered) * CAP + place
    arrives = where[None, :] == jnp.arange(2 * SIDE * SIDE * CAP, dtype=jnp.int32)[:, None]
    goes = jnp.sum(jnp.where(arrives, 1 + jnp.arange(slots_dev, dtype=jnp.int32)[None, :], 0), axis=1) - 1
    return send.reshape(-1), goes


def per_device(b_three, metric, aux_map, domains, counts):
    rows_dev, aux_dev = b_three.shape
    blocks_dev, _ = aux_map.shape
    width = rows_dev // blocks_dev
    n_pair = lax.axis_size("pair")
    n_aux = lax.axis_size("aux")
    own = lax.axis_index("pair")
    pairs_dev = counts.shape[0]
    domain_max = domains.shape[1]
    params = pltpu.CompilerParams(vmem_limit_bytes=VMEM_LIMIT)
    in_hbm = pl.BlockSpec(memory_space=pltpu.HBM)
    in_vmem = pl.BlockSpec(memory_space=pltpu.VMEM)

    place = lax.axis_index("aux").astype(jnp.int32).reshape(1)

    masked = pl.pallas_call(
        mask_kernel,
        in_specs=[in_hbm] * 2,
        out_specs=[in_vmem] * len(CHUNKS),
        scratch_shapes=[
            pltpu.VMEM(aux_map.shape, jnp.int32),
            pltpu.VMEM(b_three.shape, jnp.bfloat16),
            pltpu.SemaphoreType.DMA((2,)),
        ],
        out_shape=[jax.ShapeDtypeStruct((blocks * width, aux_dev), jnp.bfloat16) for blocks in CHUNKS],
        compiler_params=params,
        name="mask",
    )(aux_map, b_three)
    send, goes = plan(domains, own, pairs_dev, blocks_dev, n_pair)

    block_shape = (width, aux_dev)
    orders = tuple(range(n_aux))
    ordered = pl.pallas_call(
        functools.partial(metric_kernel, orders),
        grid_spec=pltpu.PrefetchScalarGridSpec(
            num_scalar_prefetch=1,
            grid=(),
            in_specs=[in_hbm],
            out_specs=in_vmem,
            scratch_shapes=[pltpu.SemaphoreType.DMA((n_aux,))],
        ),
        out_shape=jax.ShapeDtypeStruct((n_aux, aux_dev, aux_dev), jnp.bfloat16),
        compiler_params=params,
        name="order_metric",
    )(place, metric)
    rings = ring_gather(masked)
    near = tuple(hop for hop in orders if min(hop, n_aux - hop) <= n_aux // 4)
    far = tuple(hop for hop in orders if hop not in near)
    begun = pl.pallas_call(
        functools.partial(fit_kernel, near, False),
        in_specs=[in_vmem] * (len(near) * len(CHUNKS) + 1),
        out_specs=in_vmem,
        scratch_shapes=[pltpu.VMEM((max(CHUNKS) * width, aux_dev), jnp.float32)],
        out_shape=jax.ShapeDtypeStruct((rows_dev, aux_dev), jnp.float32),
        compiler_params=params,
        name="fit_near",
    )(*[ring[hop] for ring in rings for hop in near], ordered)
    fitted = pl.pallas_call(
        functools.partial(fit_kernel, far, True),
        in_specs=[in_vmem] * (len(far) * len(CHUNKS) + 2),
        out_specs=in_vmem,
        scratch_shapes=[pltpu.VMEM((max(CHUNKS) * width, aux_dev), jnp.float32)],
        out_shape=jax.ShapeDtypeStruct((blocks_dev, *block_shape), jnp.bfloat16),
        compiler_params=params,
        name="fit_far",
    )(begun, *[ring[hop] for ring in rings for hop in far], ordered)
    sources = {hop: lax.ppermute(fitted, "pair", gather_perm(hop)) for hop in GATHER_HOPS if hop > 0}
    sources[0] = fitted

    messages, slots = 2 * SIDE, SIDE * CAP
    order = tuple(hop * 2 + flip for hop, flip in SPREAD_ORDER)
    picked = []
    for start in range(0, messages, PICK_GROUP):
        group = order[start : start + PICK_GROUP]
        picked += pl.pallas_call(
            functools.partial(pick_kernel, group),
            grid_spec=pltpu.PrefetchScalarGridSpec(
                num_scalar_prefetch=1,
                grid=(),
                in_specs=[in_vmem] * SIDE,
                out_specs=[in_vmem] * len(group),
            ),
            out_shape=[jax.ShapeDtypeStruct((slots, *block_shape), jnp.bfloat16)] * len(group),
            compiler_params=params,
            name="pick",
        )(send, *[sources[hop] for hop in GATHER_HOPS])
    arrived = [
        lax.ppermute(message, "pair", spread_perm(hop, flip)) if (hop, flip) != (0, 0) else message
        for (hop, flip), message in zip(SPREAD_ORDER, picked)
    ]

    size = domain_max * width
    share = size // n_aux
    half = pairs_dev // 2
    partial_values = [
        pl.pallas_call(
            functools.partial(gram_kernel, first_pair, domain_max, order),
            grid_spec=pltpu.PrefetchScalarGridSpec(
                num_scalar_prefetch=3,
                grid=(),
                in_specs=[in_vmem] * messages,
                out_specs=in_vmem,
                scratch_shapes=[pltpu.VMEM((half * domain_max, *block_shape), jnp.bfloat16)],
            ),
            out_shape=jax.ShapeDtypeStruct((n_aux, half, share, size), jnp.float32),
            compiler_params=params,
            name="gram",
        )(goes, counts, place, *arrived)
        for first_pair in (0, half)
    ]
    return jnp.concatenate(ring_sum(partial_values), axis=0)


def solution(mesh):
    return jax.shard_map(
        per_device,
        mesh=mesh,
        in_specs=(P("pair", "aux"), P(None, "aux"), P("pair", "aux"), P(), P("pair")),
        out_specs=P("pair", "aux", None),
        check_vma=False,
    )
```

```python
import functools

import jax
import jax.numpy as jnp
from jax import lax
from jax.experimental import pallas as pl
from jax.experimental.pallas import tpu as pltpu
from jax.sharding import PartitionSpec as P

VMEM_LIMIT = 12 * 1024 * 1024
CHUNKS = (5, 3)
PAIR_CHUNKS = (5, 5)
SIDE = 4
GATHER_HOPS = (1, 3, 2, 0)
SPREAD_ORDER = ((1, 0), (3, 0), (2, 0), (1, 1), (3, 1), (2, 1), (0, 1), (0, 0))
PICK_GROUP = 2
CAP = 2


def mask_kernel(keep_ref, b_ref, *out_refs):
    width = b_ref.shape[0] // keep_ref.shape[0]
    block = 0
    for out_ref in out_refs:
        for start in range(0, out_ref.shape[0], width):
            out_ref[start : start + width, :] = b_ref[
                block * width : (block + 1) * width, :
            ] * keep_ref[block : block + 1, :].astype(jnp.bfloat16)
            block += 1


def metric_kernel(hops, own_ref, w_ref, out_ref, sems):
    steps = len(hops)
    depth = out_ref.shape[1]
    loads = []
    for step, hop in enumerate(hops):
        row = pl.multiple_of(((own_ref[0] + steps - hop) % steps) * depth, depth)
        loads.append(pltpu.make_async_copy(w_ref.at[pl.ds(row, depth)], out_ref.at[step], sems.at[step]))
    for load in loads:
        load.start()
    for load in loads:
        load.wait()


def fit_kernel(*refs):
    pieces, w_ref, out_ref, total = refs[:-3], refs[-3], refs[-2], refs[-1]
    for step, piece in enumerate(pieces):
        part = jnp.dot(piece[...], w_ref[step], preferred_element_type=jnp.float32)
        if step == 0:
            total[...] = part
        elif step < len(pieces) - 1:
            total[...] += part
        else:
            out_ref[...] = (total[...] + part).astype(jnp.bfloat16).reshape(out_ref.shape)


def pick_kernel(messages, send_ref, *refs):
    count = SIDE * len(CHUNKS)
    sources, outs = refs[:count], refs[count:]
    hop_of = {hop: index for index, hop in enumerate(GATHER_HOPS)}
    for message, out in zip(messages, outs):
        slots = out.shape[0]
        for slot in range(slots):
            block = send_ref[message * slots + slot]
            first = 0
            for chunk, blocks in enumerate(CHUNKS):
                source = sources[hop_of[slot // CAP] * len(CHUNKS) + chunk]

                @pl.when((block >= first) & (block < first + blocks))
                def _(out=out, slot=slot, source=source, index=block - first):
                    out[slot] = source[index]

                first += blocks


def add_kernel(index, a_ref, part_ref, out_ref):
    out_ref[...] = a_ref[...] + part_ref[index]


def last_kernel(*refs):
    refs, out_ref = refs[:-1], refs[-1]
    row = 0
    for index in range(0, len(refs), 3):
        part, right, left = refs[index : index + 3]
        pairs = part.shape[1]
        out_ref[row : row + pairs] = part[0] + right[...] + left[...]
        row += pairs


def gram_kernel(first_pair, domain_max, order, goes_ref, counts_ref, own_ref, *refs):
    arrived, out_ref, stacks = refs[:-2], refs[-2], refs[-1]
    slots = arrived[0].shape[0]
    n_aux, pairs, share, size = out_ref.shape
    places, width, depth = stacks.shape
    for message, source in zip(order, arrived):
        for slot in range(slots):
            goes = goes_ref[message * slots + slot] - first_pair * domain_max

            @pl.when((goes >= 0) & (goes < places))
            def _(source=source, slot=slot, goes=goes):
                stacks[goes] = source[slot]

    row = lax.broadcasted_iota(jnp.int32, (size, size), 0)
    column = lax.broadcasted_iota(jnp.int32, (size, size), 1)
    furthest = jnp.maximum(row, column)
    for pair in range(pairs):
        stack = stacks[pair * domain_max : (pair + 1) * domain_max].reshape(size, depth)
        value = lax.dot_general(
            stack, stack, (((1,), (1,)), ((), ())), preferred_element_type=jnp.float32
        )
        value = jnp.where(furthest < counts_ref[first_pair + pair] * width, value, 0.0)
        value = value.reshape(n_aux, share, size)
        for index in range(n_aux):
            out_ref[(index + n_aux - own_ref[0]) % n_aux, pair] = value[index]


def ring_gather(chunks, early):
    n_aux = lax.axis_size("aux")
    rings = []
    for index, chunk in enumerate(chunks):
        far = n_aux // 2 if index % 2 == 0 else n_aux // 2 - 1
        rings.append((far, n_aux - 1 - far, {0: chunk}, [chunk, chunk]))
    for step in range(1, n_aux // 2 + 1):
        before = None
        for far_right, far_left, found, moving in rings:
            arrived = list(moving)
            for side, (by, far) in enumerate(((1, far_right), (-1, far_left))):
                if step <= far:
                    if before is not None and step > 1:
                        moving[side], _ = lax.optimization_barrier((moving[side], before[side]))
                    moving[side] = shift(moving[side], by)
                    found[step * by % n_aux] = moving[side]
            before = arrived
        if step == 1:
            moving[0], early = lax.optimization_barrier((moving[0], early))
    return [found for _, _, found, _ in rings], early


def ring_sum(parts):
    n_aux = lax.axis_size("aux")
    rings = []
    for index, part in enumerate(parts):
        far = n_aux // 2 if index % 2 == 0 else n_aux // 2 - 1
        rings.append([part, far, n_aux - 1 - far, None, None])
    for step in range(n_aux // 2, 0, -1):
        for ring in rings:
            part, far_right, far_left, right, left = ring
            if step <= far_right:
                ring[3] = shift(part[step] if right is None else add_term(right, part, step), 1)
            if step <= far_left:
                ring[4] = shift(part[n_aux - step] if left is None else add_term(left, part, n_aux - step), -1)
    parts_moved = [value for part, _, _, right, left in rings for value in (part, right, left)]
    pairs = [part.shape[1] for part in parts]
    in_vmem = pl.BlockSpec(memory_space=pltpu.VMEM)
    return pl.pallas_call(
        last_kernel,
        in_specs=[in_vmem] * len(parts_moved),
        out_specs=in_vmem,
        out_shape=jax.ShapeDtypeStruct((sum(pairs), *parts[0].shape[2:]), parts[0].dtype),
        compiler_params=pltpu.CompilerParams(vmem_limit_bytes=VMEM_LIMIT),
        name="last_terms",
    )(*parts_moved)


def add_term(moving, part, index):
    in_vmem = pl.BlockSpec(memory_space=pltpu.VMEM)
    return pl.pallas_call(
        functools.partial(add_kernel, index),
        in_specs=[in_vmem] * 2,
        out_specs=in_vmem,
        out_shape=jax.ShapeDtypeStruct(moving.shape, moving.dtype),
        compiler_params=pltpu.CompilerParams(vmem_limit_bytes=VMEM_LIMIT),
        name="add_term",
    )(moving, part)


def shift(value, by):
    n_aux = lax.axis_size("aux")
    return lax.ppermute(value, "aux", [(index, (index + by) % n_aux) for index in range(n_aux)])


def device_of(x, y, core):
    return (x % SIDE) * 2 * SIDE + (y % SIDE) * 2 + core % 2


def gather_perm(hop):
    return [
        (device_of(x, y, core), device_of(x + hop, y, 0) if core == 0 else device_of(x, y + hop, 1))
        for x in range(SIDE)
        for y in range(SIDE)
        for core in range(2)
    ]


def spread_perm(hop, flip):
    return [
        (
            device_of(x, y, core),
            device_of(x, y + hop, flip) if core == 0 else device_of(x + hop, y, 1 - flip),
        )
        for x in range(SIDE)
        for y in range(SIDE)
        for core in range(2)
    ]


def plan(domains, own, pairs_dev, blocks_dev, n_pair):
    table = domains.reshape(n_pair, pairs_dev * domains.shape[1])
    slots_dev = table.shape[1]
    x, y, core = own // (2 * SIDE), (own // 2) % SIDE, own % 2
    first = core == 0
    hops = jnp.arange(SIDE, dtype=jnp.int32)
    flips = jnp.arange(2, dtype=jnp.int32)
    source = jnp.where(first, device_of(x - hops, y, 0), device_of(x, y - hops, 1))
    target = jnp.where(
        first,
        device_of(x, y + hops[:, None], flips[None, :]),
        device_of(x + hops[:, None], y, 1 - flips[None, :]),
    ).reshape(2 * SIDE)

    chosen = jnp.concatenate([target, own[None]])[:, None] == jnp.arange(n_pair, dtype=jnp.int32)[None, :]
    rows = jnp.sum(jnp.where(chosen[:, :, None], table[None], 0), axis=1)
    owner, local = rows // blocks_dev, rows % blocks_dev
    earlier = jnp.tril(jnp.ones((slots_dev, slots_dev), jnp.bool_), -1)
    rank = jnp.sum(((owner[:, :, None] == owner[:, None, :]) & earlier[None]).astype(jnp.int32), axis=2)
    key = owner * CAP + rank
    wanted = (source[:, None] * CAP + jnp.arange(CAP, dtype=jnp.int32)[None, :]).reshape(SIDE * CAP)
    hit = key[:-1, None, :] == wanted[None, :, None]
    send = jnp.sum(jnp.where(hit, local[:-1, None, :], 0), axis=2)

    named, place = owner[-1], rank[-1]
    back_x, back_y = (x - named // (2 * SIDE)) % SIDE, (y - (named // 2) % SIDE) % SIDE
    sent_first = named % 2 == 0
    gathered = jnp.where(sent_first, back_x, back_y)
    spread = jnp.where(sent_first, back_y, back_x)
    flip = jnp.where(sent_first, core, 1 - core)
    where = ((spread * 2 + flip) * SIDE + gathered) * CAP + place
    arrives = where[None, :] == jnp.arange(2 * SIDE * SIDE * CAP, dtype=jnp.int32)[:, None]
    goes = jnp.sum(jnp.where(arrives, 1 + jnp.arange(slots_dev, dtype=jnp.int32)[None, :], 0), axis=1) - 1
    return send.reshape(-1), goes


def per_device(b_three, metric, aux_map, domains, counts):
    rows_dev, aux_dev = b_three.shape
    blocks_dev, _ = aux_map.shape
    width = rows_dev // blocks_dev
    n_pair = lax.axis_size("pair")
    n_aux = lax.axis_size("aux")
    own = lax.axis_index("pair")
    pairs_dev = counts.shape[0]
    domain_max = domains.shape[1]
    params = pltpu.CompilerParams(vmem_limit_bytes=VMEM_LIMIT)
    in_hbm = pl.BlockSpec(memory_space=pltpu.HBM)
    in_vmem = pl.BlockSpec(memory_space=pltpu.VMEM)

    place = lax.axis_index("aux").astype(jnp.int32).reshape(1)

    aux_block = jnp.arange(aux_dev, dtype=jnp.int32) // (aux_dev // aux_map.shape[1])
    inside = jnp.arange(aux_map.shape[1], dtype=jnp.int32)[:, None] == aux_block[None, :]
    keep = jnp.sum(jnp.where(inside[None], aux_map[:, :, None], 0), axis=1).astype(jnp.float32)
    masked = pl.pallas_call(
        mask_kernel,
        in_specs=[in_vmem] * 2,
        out_specs=[in_vmem] * len(CHUNKS),
        out_shape=[jax.ShapeDtypeStruct((blocks * width, aux_dev), jnp.bfloat16) for blocks in CHUNKS],
        compiler_params=params,
        name="mask",
    )(keep, b_three)
    send, goes = plan(domains, own, pairs_dev, blocks_dev, n_pair)

    block_shape = (width, aux_dev)
    orders = tuple(range(n_aux))
    ordered = pl.pallas_call(
        functools.partial(metric_kernel, orders),
        grid_spec=pltpu.PrefetchScalarGridSpec(
            num_scalar_prefetch=1,
            grid=(),
            in_specs=[in_hbm],
            out_specs=in_vmem,
            scratch_shapes=[pltpu.SemaphoreType.DMA((n_aux,))],
        ),
        out_shape=jax.ShapeDtypeStruct((n_aux, aux_dev, aux_dev), jnp.bfloat16),
        compiler_params=params,
        name="order_metric",
    )(place, metric)
    rings, ordered = ring_gather(masked, ordered)
    sources = {}
    for index, (blocks, ring) in enumerate(zip(CHUNKS, rings)):
        fitted = pl.pallas_call(
            fit_kernel,
            in_specs=[in_vmem] * (n_aux + 1),
            out_specs=in_vmem,
            scratch_shapes=[pltpu.VMEM((blocks * width, aux_dev), jnp.float32)],
            out_shape=jax.ShapeDtypeStruct((blocks, *block_shape), jnp.bfloat16),
            compiler_params=params,
            name="fit",
        )(*[ring[hop] for hop in orders], ordered)
        for hop in GATHER_HOPS:
            sources[hop, index] = lax.ppermute(fitted, "pair", gather_perm(hop)) if hop > 0 else fitted

    messages, slots = 2 * SIDE, SIDE * CAP
    order = tuple(hop * 2 + flip for hop, flip in SPREAD_ORDER)
    picked = []
    for start in range(0, messages, PICK_GROUP):
        group = order[start : start + PICK_GROUP]
        picked += pl.pallas_call(
            functools.partial(pick_kernel, group),
            grid_spec=pltpu.PrefetchScalarGridSpec(
                num_scalar_prefetch=1,
                grid=(),
                in_specs=[in_vmem] * (SIDE * len(CHUNKS)),
                out_specs=[in_vmem] * len(group),
            ),
            out_shape=[jax.ShapeDtypeStruct((slots, *block_shape), jnp.bfloat16)] * len(group),
            compiler_params=params,
            name="pick",
        )(send, *[sources[hop, index] for hop in GATHER_HOPS for index in range(len(CHUNKS))])
    arrived = [
        lax.ppermute(message, "pair", spread_perm(hop, flip)) if (hop, flip) != (0, 0) else message
        for (hop, flip), message in zip(SPREAD_ORDER, picked)
    ]

    size = domain_max * width
    share = size // n_aux
    partial_values = []
    first_pair = 0
    for pairs in PAIR_CHUNKS:
        partial_values.append(
            pl.pallas_call(
                functools.partial(gram_kernel, first_pair, domain_max, order),
                grid_spec=pltpu.PrefetchScalarGridSpec(
                    num_scalar_prefetch=3,
                    grid=(),
                    in_specs=[in_vmem] * messages,
                    out_specs=in_vmem,
                    scratch_shapes=[pltpu.VMEM((pairs * domain_max, *block_shape), jnp.bfloat16)],
                ),
                out_shape=jax.ShapeDtypeStruct((n_aux, pairs, share, size), jnp.float32),
                compiler_params=params,
                name="gram",
            )(goes, counts, place, *arrived)
        )
        first_pair += pairs
    return ring_sum(partial_values)


def solution(mesh):
    return jax.shard_map(
        per_device,
        mesh=mesh,
        in_specs=(P("pair", "aux"), P(None, "aux"), P("pair", "aux"), P(), P("pair")),
        out_specs=P("pair", "aux", None),
        check_vma=False,
    )
```

```python
import functools

import jax
import jax.numpy as jnp
from jax import lax
from jax.experimental import pallas as pl
from jax.experimental.pallas import tpu as pltpu
from jax.sharding import PartitionSpec as P

VMEM_LIMIT = 12 * 1024 * 1024
CHUNKS = (5, 3)
PAIR_CHUNKS = (5, 5)
SIDE = 4
GATHER_HOPS = (1, 3, 2, 0)
SPREAD_ORDER = ((1, 0), (3, 0), (1, 1), (3, 1), (2, 0), (2, 1), (0, 1), (0, 0))
PICK_GROUP = 2
CAP = 2


def mask_kernel(keep_ref, b_ref, *out_refs):
    width = b_ref.shape[0] // keep_ref.shape[0]
    block = 0
    for out_ref in out_refs:
        for start in range(0, out_ref.shape[0], width):
            out_ref[start : start + width, :] = b_ref[
                block * width : (block + 1) * width, :
            ] * keep_ref[block : block + 1, :].astype(jnp.bfloat16)
            block += 1


def metric_kernel(hops, own_ref, w_ref, out_ref, sems):
    steps = len(hops)
    depth = out_ref.shape[1]
    loads = []
    for step, hop in enumerate(hops):
        row = pl.multiple_of(((own_ref[0] + steps - hop) % steps) * depth, depth)
        loads.append(pltpu.make_async_copy(w_ref.at[pl.ds(row, depth)], out_ref.at[step], sems.at[step]))
    for load in loads:
        load.start()
    for load in loads:
        load.wait()


def fit_kernel(*refs):
    pieces, w_ref, out_ref, total = refs[:-3], refs[-3], refs[-2], refs[-1]
    for step, piece in enumerate(pieces):
        part = jnp.dot(piece[...], w_ref[step], preferred_element_type=jnp.float32)
        if step == 0:
            total[...] = part
        elif step < len(pieces) - 1:
            total[...] += part
        else:
            out_ref[...] = (total[...] + part).astype(jnp.bfloat16).reshape(out_ref.shape)


def pick_kernel(messages, send_ref, *refs):
    count = SIDE * len(CHUNKS)
    sources, outs = refs[:count], refs[count:]
    hop_of = {hop: index for index, hop in enumerate(GATHER_HOPS)}
    for message, out in zip(messages, outs):
        slots = out.shape[0]
        for slot in range(slots):
            block = send_ref[message * slots + slot]
            first = 0
            for chunk, blocks in enumerate(CHUNKS):
                source = sources[hop_of[slot // CAP] * len(CHUNKS) + chunk]

                @pl.when((block >= first) & (block < first + blocks))
                def _(out=out, slot=slot, source=source, index=block - first):
                    out[slot] = source[index]

                first += blocks


def add_kernel(index, a_ref, part_ref, out_ref):
    out_ref[...] = a_ref[...] + part_ref[index]


def last_kernel(*refs):
    refs, out_ref = refs[:-1], refs[-1]
    row = 0
    for index in range(0, len(refs), 3):
        part, right, left = refs[index : index + 3]
        pairs = part.shape[1]
        out_ref[row : row + pairs] = part[0] + right[...] + left[...]
        row += pairs


def gram_kernel(first_pair, domain_max, order, goes_ref, counts_ref, own_ref, *refs):
    arrived, out_ref, stacks = refs[:-2], refs[-2], refs[-1]
    slots = arrived[0].shape[0]
    n_aux, pairs, share, size = out_ref.shape
    places, width, depth = stacks.shape
    for message, source in zip(order, arrived):
        for slot in range(slots):
            goes = goes_ref[message * slots + slot] - first_pair * domain_max

            @pl.when((goes >= 0) & (goes < places))
            def _(source=source, slot=slot, goes=goes):
                stacks[goes] = source[slot]

    row = lax.broadcasted_iota(jnp.int32, (size, size), 0)
    column = lax.broadcasted_iota(jnp.int32, (size, size), 1)
    furthest = jnp.maximum(row, column)
    for pair in range(pairs):
        stack = stacks[pair * domain_max : (pair + 1) * domain_max].reshape(size, depth)
        value = lax.dot_general(
            stack, stack, (((1,), (1,)), ((), ())), preferred_element_type=jnp.float32
        )
        value = jnp.where(furthest < counts_ref[first_pair + pair] * width, value, 0.0)
        value = value.reshape(n_aux, share, size)
        for index in range(n_aux):
            out_ref[(index + n_aux - own_ref[0]) % n_aux, pair] = value[index]


def ring_gather(chunks, early):
    n_aux = lax.axis_size("aux")
    rings = []
    for index, chunk in enumerate(chunks):
        far = n_aux // 2 if index % 2 == 0 else n_aux // 2 - 1
        rings.append((far, n_aux - 1 - far, {0: chunk}, [chunk, chunk]))
    for step in range(1, n_aux // 2 + 1):
        before = None
        for far_right, far_left, found, moving in rings:
            arrived = list(moving)
            for side, (by, far) in enumerate(((1, far_right), (-1, far_left))):
                if step <= far:
                    if before is not None and step > 1:
                        moving[side], _ = lax.optimization_barrier((moving[side], before[side]))
                    moving[side] = shift(moving[side], by)
                    found[step * by % n_aux] = moving[side]
            before = arrived
        if step == 1:
            moving[0], early = lax.optimization_barrier((moving[0], early))
    return [found for _, _, found, _ in rings], early


def ring_sum(parts):
    n_aux = lax.axis_size("aux")
    rings = []
    for index, part in enumerate(parts):
        far = n_aux // 2 if index % 2 == 0 else n_aux // 2 - 1
        rings.append([part, far, n_aux - 1 - far, None, None])
    for step in range(n_aux // 2, 0, -1):
        for ring in rings:
            part, far_right, far_left, right, left = ring
            if step <= far_right:
                ring[3] = shift(part[step] if right is None else add_term(right, part, step), 1)
            if step <= far_left:
                ring[4] = shift(part[n_aux - step] if left is None else add_term(left, part, n_aux - step), -1)
    parts_moved = [value for part, _, _, right, left in rings for value in (part, right, left)]
    pairs = [part.shape[1] for part in parts]
    in_vmem = pl.BlockSpec(memory_space=pltpu.VMEM)
    return pl.pallas_call(
        last_kernel,
        in_specs=[in_vmem] * len(parts_moved),
        out_specs=in_vmem,
        out_shape=jax.ShapeDtypeStruct((sum(pairs), *parts[0].shape[2:]), parts[0].dtype),
        compiler_params=pltpu.CompilerParams(vmem_limit_bytes=VMEM_LIMIT),
        name="last_terms",
    )(*parts_moved)


def add_term(moving, part, index):
    in_vmem = pl.BlockSpec(memory_space=pltpu.VMEM)
    return pl.pallas_call(
        functools.partial(add_kernel, index),
        in_specs=[in_vmem] * 2,
        out_specs=in_vmem,
        out_shape=jax.ShapeDtypeStruct(moving.shape, moving.dtype),
        compiler_params=pltpu.CompilerParams(vmem_limit_bytes=VMEM_LIMIT),
        name="add_term",
    )(moving, part)


def shift(value, by):
    n_aux = lax.axis_size("aux")
    return lax.ppermute(value, "aux", [(index, (index + by) % n_aux) for index in range(n_aux)])


def device_of(x, y, core):
    return (x % SIDE) * 2 * SIDE + (y % SIDE) * 2 + core % 2


def gather_perm(hop):
    return [
        (device_of(x, y, core), device_of(x + hop, y, 0) if core == 0 else device_of(x, y + hop, 1))
        for x in range(SIDE)
        for y in range(SIDE)
        for core in range(2)
    ]


def spread_perm(hop, flip):
    return [
        (
            device_of(x, y, core),
            device_of(x, y + hop, flip) if core == 0 else device_of(x + hop, y, 1 - flip),
        )
        for x in range(SIDE)
        for y in range(SIDE)
        for core in range(2)
    ]


def plan(domains, own, pairs_dev, blocks_dev, n_pair):
    table = domains.reshape(n_pair, pairs_dev * domains.shape[1])
    slots_dev = table.shape[1]
    x, y, core = own // (2 * SIDE), (own // 2) % SIDE, own % 2
    first = core == 0
    hops = jnp.arange(SIDE, dtype=jnp.int32)
    flips = jnp.arange(2, dtype=jnp.int32)
    source = jnp.where(first, device_of(x - hops, y, 0), device_of(x, y - hops, 1))
    target = jnp.where(
        first,
        device_of(x, y + hops[:, None], flips[None, :]),
        device_of(x + hops[:, None], y, 1 - flips[None, :]),
    ).reshape(2 * SIDE)

    chosen = jnp.concatenate([target, own[None]])[:, None] == jnp.arange(n_pair, dtype=jnp.int32)[None, :]
    rows = jnp.sum(jnp.where(chosen[:, :, None], table[None], 0), axis=1)
    owner, local = rows // blocks_dev, rows % blocks_dev
    earlier = jnp.tril(jnp.ones((slots_dev, slots_dev), jnp.bool_), -1)
    rank = jnp.sum(((owner[:, :, None] == owner[:, None, :]) & earlier[None]).astype(jnp.int32), axis=2)
    key = owner * CAP + rank
    wanted = (source[:, None] * CAP + jnp.arange(CAP, dtype=jnp.int32)[None, :]).reshape(SIDE * CAP)
    hit = key[:-1, None, :] == wanted[None, :, None]
    send = jnp.sum(jnp.where(hit, local[:-1, None, :], 0), axis=2)

    named, place = owner[-1], rank[-1]
    back_x, back_y = (x - named // (2 * SIDE)) % SIDE, (y - (named // 2) % SIDE) % SIDE
    sent_first = named % 2 == 0
    gathered = jnp.where(sent_first, back_x, back_y)
    spread = jnp.where(sent_first, back_y, back_x)
    flip = jnp.where(sent_first, core, 1 - core)
    where = ((spread * 2 + flip) * SIDE + gathered) * CAP + place
    arrives = where[None, :] == jnp.arange(2 * SIDE * SIDE * CAP, dtype=jnp.int32)[:, None]
    goes = jnp.sum(jnp.where(arrives, 1 + jnp.arange(slots_dev, dtype=jnp.int32)[None, :], 0), axis=1) - 1
    return send.reshape(-1), goes


def per_device(b_three, metric, aux_map, domains, counts):
    rows_dev, aux_dev = b_three.shape
    blocks_dev, _ = aux_map.shape
    width = rows_dev // blocks_dev
    n_pair = lax.axis_size("pair")
    n_aux = lax.axis_size("aux")
    own = lax.axis_index("pair")
    pairs_dev = counts.shape[0]
    domain_max = domains.shape[1]
    params = pltpu.CompilerParams(vmem_limit_bytes=VMEM_LIMIT)
    in_hbm = pl.BlockSpec(memory_space=pltpu.HBM)
    in_vmem = pl.BlockSpec(memory_space=pltpu.VMEM)

    place = lax.axis_index("aux").astype(jnp.int32).reshape(1)

    aux_block = jnp.arange(aux_dev, dtype=jnp.int32) // (aux_dev // aux_map.shape[1])
    inside = jnp.arange(aux_map.shape[1], dtype=jnp.int32)[:, None] == aux_block[None, :]
    keep = jnp.sum(jnp.where(inside[None], aux_map[:, :, None], 0), axis=1).astype(jnp.float32)
    masked = pl.pallas_call(
        mask_kernel,
        in_specs=[in_vmem] * 2,
        out_specs=[in_vmem] * len(CHUNKS),
        out_shape=[jax.ShapeDtypeStruct((blocks * width, aux_dev), jnp.bfloat16) for blocks in CHUNKS],
        compiler_params=params,
        name="mask",
    )(keep, b_three)
    send, goes = plan(domains, own, pairs_dev, blocks_dev, n_pair)

    block_shape = (width, aux_dev)
    orders = tuple(range(n_aux))
    ordered = pl.pallas_call(
        functools.partial(metric_kernel, orders),
        grid_spec=pltpu.PrefetchScalarGridSpec(
            num_scalar_prefetch=1,
            grid=(),
            in_specs=[in_hbm],
            out_specs=in_vmem,
            scratch_shapes=[pltpu.SemaphoreType.DMA((n_aux,))],
        ),
        out_shape=jax.ShapeDtypeStruct((n_aux, aux_dev, aux_dev), jnp.bfloat16),
        compiler_params=params,
        name="order_metric",
    )(place, metric)
    rings, ordered = ring_gather(masked, ordered)
    sources = {}
    for index, (blocks, ring) in enumerate(zip(CHUNKS, rings)):
        fitted = pl.pallas_call(
            fit_kernel,
            in_specs=[in_vmem] * (n_aux + 1),
            out_specs=in_vmem,
            scratch_shapes=[pltpu.VMEM((blocks * width, aux_dev), jnp.float32)],
            out_shape=jax.ShapeDtypeStruct((blocks, *block_shape), jnp.bfloat16),
            compiler_params=params,
            name="fit",
        )(*[ring[hop] for hop in orders], ordered)
        for hop in GATHER_HOPS:
            sources[hop, index] = lax.ppermute(fitted, "pair", gather_perm(hop)) if hop > 0 else fitted

    messages, slots = 2 * SIDE, SIDE * CAP
    order = tuple(hop * 2 + flip for hop, flip in SPREAD_ORDER)
    picked = []
    for start in range(0, messages, PICK_GROUP):
        group = order[start : start + PICK_GROUP]
        picked += pl.pallas_call(
            functools.partial(pick_kernel, group),
            grid_spec=pltpu.PrefetchScalarGridSpec(
                num_scalar_prefetch=1,
                grid=(),
                in_specs=[in_vmem] * (SIDE * len(CHUNKS)),
                out_specs=[in_vmem] * len(group),
            ),
            out_shape=[jax.ShapeDtypeStruct((slots, *block_shape), jnp.bfloat16)] * len(group),
            compiler_params=params,
            name="pick",
        )(send, *[sources[hop, index] for hop in GATHER_HOPS for index in range(len(CHUNKS))])
    arrived = [
        lax.ppermute(message, "pair", spread_perm(hop, flip)) if (hop, flip) != (0, 0) else message
        for (hop, flip), message in zip(SPREAD_ORDER, picked)
    ]

    size = domain_max * width
    share = size // n_aux
    partial_values = []
    first_pair = 0
    for pairs in PAIR_CHUNKS:
        partial_values.append(
            pl.pallas_call(
                functools.partial(gram_kernel, first_pair, domain_max, order),
                grid_spec=pltpu.PrefetchScalarGridSpec(
                    num_scalar_prefetch=3,
                    grid=(),
                    in_specs=[in_vmem] * messages,
                    out_specs=in_vmem,
                    scratch_shapes=[pltpu.VMEM((pairs * domain_max, *block_shape), jnp.bfloat16)],
                ),
                out_shape=jax.ShapeDtypeStruct((n_aux, pairs, share, size), jnp.float32),
                compiler_params=params,
                name="gram",
            )(goes, counts, place, *arrived)
        )
        first_pair += pairs
    return ring_sum(partial_values)


def solution(mesh):
    return jax.shard_map(
        per_device,
        mesh=mesh,
        in_specs=(P("pair", "aux"), P(None, "aux"), P("pair", "aux"), P(), P("pair")),
        out_specs=P("pair", "aux", None),
        check_vma=False,
    )
```
